256 devices in a mesh: pipe: 8 (over z_hi, core), expert: 32 (over z_lo, y, x).
Axes of the slice: x: 4, y: 4, z: 8 (z_hi: 4, z_lo: 2; z = z_hi * 2 + z_lo), core: 2. Of those that a mesh axis runs over, the one named last changes fastest.
Arguments:
- forward_in: bfloat16 [8, 4096, 4096], P('pipe', 'expert'), may hold values from -6 to 6
- forward_route: int32 [8, 4096, 1], P('pipe', 'expert'), may hold values from 0 to 7, as said below
- forward_gate_prob: float32 [8, 4096, 1], P('pipe', 'expert'), may hold values from 0.25 to 1
- backward_in: bfloat16 [8, 4096, 4096], P('pipe', 'expert'), may hold values from -6 to 6
- backward_route: int32 [8, 4096, 1], P('pipe', 'expert'), may hold values from 0 to 7, as said below
- backward_gate_prob: float32 [8, 4096, 1], P('pipe', 'expert'), may hold values from 0.25 to 1
- cotangent: bfloat16 [8, 4096, 4096], P('pipe', 'expert'), may hold values from -6 to 6
- w_gate: bfloat16 [8, 4096, 8192], P('pipe', None, 'expert'), may hold values from -0.09375 to 0.09375
- w_up: bfloat16 [8, 4096, 8192], P('pipe', None, 'expert'), may hold values from -0.09375 to 0.09375
- w_down: bfloat16 [8, 8192, 4096], P('pipe', 'expert'), may hold values from -0.1875 to 0.1875
Outputs:
- next_forward: bfloat16 [8, 4096, 4096], P('pipe', 'expert')
- next_cotangent: bfloat16 [8, 4096, 4096], P('pipe', 'expert')
The draws below stay inside these ranges and needn't reach their ends.
Inputs may be any that keep to these rules, and one draw needn't show every extreme that they name: `forward_route`: among the 128 tokens of one device at one section no expert is named more than 20 times; in each section one expert is named exactly 20 times by every device's tokens. `backward_route`: among the 128 tokens of one device at one section no expert is named more than 20 times; in each section one expert is named exactly 20 times by every device's tokens.
All inputs are finite; a program needn't handle non-finite values.
Results may differ from the reference program's by a relative error of at most 0.0095.
Values may be sent and summed in bfloat16 or wider, within the bound.
A program may use at most 128 MiB of HBM per device.

```python
import jax
import jax.numpy as jnp
from jax import lax

D = 4096
HID = 1024
GROUP = 4
TOP = 1
TOK_DEV = 128
HDEV = 256
EXPERTS = 8
TOKENS = 4096
CAP = 20
N_PIPE = 8
N_EXPERT = 32


def route_block(block_key, full_expert):
    key_one, key_two = jax.random.split(block_key)
    others = (full_expert + 1 + jnp.arange((EXPERTS - 1) * CAP, dtype=jnp.int32) // CAP) % EXPERTS
    picked = jax.random.permutation(key_one, others)[:TOK_DEV - CAP]
    block_ids = jnp.concatenate([jnp.full((CAP,), full_expert, dtype=jnp.int32), picked.astype(jnp.int32)])
    return jax.random.permutation(key_two, block_ids)


def route_draw(base_key):
    segment_key, block_key = jax.random.split(base_key)
    chosen = jax.random.randint(segment_key, (N_PIPE,), 0, EXPERTS, dtype=jnp.int32)
    full_expert = jnp.repeat(chosen, N_EXPERT)
    block_keys = jax.random.split(block_key, N_PIPE * N_EXPERT)
    blocks = jax.vmap(route_block)(block_keys, full_expert)
    return blocks.reshape(N_PIPE, TOKENS, TOP).astype(jnp.int32)


def draw_forward_route(key, part):
    key = jax.random.fold_in(key, 11)
    return route_draw(key)


def draw_backward_route(key, part):
    key = jax.random.fold_in(key, 23)
    return route_draw(key)


def levels(stream_key, shape, cuts, low, largest):
    def one(axis_at, shards_of):
        draws = jax.random.uniform(jax.random.fold_in(jax.random.fold_in(stream_key, 6), axis_at), (shards_of,), jnp.float32, low / len(cuts), largest / len(cuts))
        return jnp.repeat(jnp.exp(draws), shape[axis_at] // shards_of).reshape((-1,) + (1,) * (len(shape) - axis_at - 1))

    loudness = one(*cuts[0])
    for cut in cuts[1:]:
        loudness = loudness * one(*cut)
    return loudness


def noise(rng, extent, width, reach, cuts=(), kind=jnp.bfloat16):
    drawn = jax.random.normal(rng, extent, jnp.float32) * width
    if len(cuts) > 0:
        drawn = levels(rng, extent, cuts, -0.22, 0.18) * drawn
    return jnp.clip(drawn, min=-reach, max=reach).astype(kind)


def setup_inputs(seed: int = 0) -> dict:
    key_of = jax.random.split(jax.random.key(seed), 11)
    forward_in = noise(key_of[0], (N_PIPE, TOKENS, D), 1.0, 6.0, ((0, 8), (1, 32)))
    forward_route = draw_forward_route(jax.random.fold_in(key_of[10], 71), 0)
    forward_gate_prob = jnp.clip(0.25 + 0.75 * jax.random.uniform(key_of[2], (N_PIPE, TOKENS, TOP), jnp.float32) ** levels(key_of[2], (N_PIPE, TOKENS, TOP), ((0, 8), (1, 32)), -0.2, 0.2), 0.25, 1.0)
    backward_in = noise(key_of[3], (N_PIPE, TOKENS, D), 1.0, 6.0, ((0, 8), (1, 32)))
    backward_route = draw_backward_route(jax.random.fold_in(key_of[10], 71), 0)
    backward_gate_prob = jnp.clip(0.25 + 0.75 * jax.random.uniform(key_of[5], (N_PIPE, TOKENS, TOP), jnp.float32) ** levels(key_of[5], (N_PIPE, TOKENS, TOP), ((0, 8), (1, 32)), -0.2, 0.2), 0.25, 1.0)
    cotangent = noise(key_of[6], (N_PIPE, TOKENS, D), 1.0, 6.0, ((0, 8), (1, 32)))
    w_gate = noise(key_of[7], (N_PIPE, D, EXPERTS * HID), D ** -0.5, 0.09375, ((0, 8), (2, 32)))
    w_up = noise(key_of[8], (N_PIPE, D, EXPERTS * HID), D ** -0.5, 0.09375, ((0, 8), (2, 32)))
    w_down = noise(key_of[9], (N_PIPE, EXPERTS * HID, D), HID ** -0.5, 0.1875, ((0, 8), (1, 32)))
    return dict(forward_in=forward_in, forward_route=forward_route, forward_gate_prob=forward_gate_prob, backward_in=backward_in, backward_route=backward_route, backward_gate_prob=backward_gate_prob, cotangent=cotangent, w_gate=w_gate, w_up=w_up, w_down=w_down)


def place_rows(expert_ids):
    onehot = (expert_ids[:, None] == jnp.arange(EXPERTS, dtype=jnp.int32)[None, :]).astype(jnp.int32)
    onehot = onehot.reshape(N_EXPERT, TOK_DEV, EXPERTS)
    before = jnp.cumsum(onehot, axis=1) - onehot
    slot_pos = jnp.sum(onehot * before, axis=2).reshape(TOKENS)
    source = jnp.arange(TOKENS, dtype=jnp.int32) // TOK_DEV
    return (expert_ids * (N_EXPERT * CAP) + source * CAP + slot_pos).astype(jnp.int32)


def fill_buffer(values, dest_rows):
    buffer = jnp.zeros((EXPERTS * N_EXPERT * CAP, D), jnp.bfloat16).at[dest_rows].set(values)
    return buffer.reshape(EXPERTS, N_EXPERT * CAP, D)


def split_weights(w_gate, w_up, w_down):
    gate_e = w_gate.reshape(D, EXPERTS, HID).transpose(1, 0, 2)
    up_e = w_up.reshape(D, EXPERTS, HID).transpose(1, 0, 2)
    down_e = w_down.reshape(EXPERTS, HID, D)
    return gate_e, up_e, down_e


def forward_segment(inputs, route_ids, gate_prob, w_gate, w_up, w_down):
    dest_rows = place_rows(route_ids)
    buffer = fill_buffer(inputs, dest_rows)
    gate_e, up_e, down_e = split_weights(w_gate, w_up, w_down)

    def expert_fwd(operands):
        in_rows, gate_w, up_w, down_w = operands
        gate_pre = jnp.dot(in_rows, gate_w, preferred_element_type=jnp.float32)
        up_pre = jnp.dot(in_rows, up_w, preferred_element_type=jnp.float32)
        hidden = (jax.nn.silu(gate_pre) * up_pre).astype(jnp.bfloat16).reshape(-1, GROUP, HDEV)
        quarters = jnp.einsum("mgh,ghd->gmd", hidden.astype(jnp.float32), down_w.reshape(GROUP, HDEV, D).astype(jnp.float32))
        return jnp.sum(quarters.astype(jnp.bfloat16).astype(jnp.float32), axis=0)

    outputs = lax.map(expert_fwd, (buffer, gate_e, up_e, down_e)).reshape(-1, D)
    branch = outputs[dest_rows]
    return (inputs.astype(jnp.float32) + gate_prob[:, None] * branch).astype(jnp.bfloat16)


def backward_segment(inputs, route_ids, gate_prob, grads, w_gate, w_up, w_down):
    dest_rows = place_rows(route_ids)
    in_buffer = fill_buffer(inputs, dest_rows)
    grad_buffer = fill_buffer(grads, dest_rows)
    gate_e, up_e, down_e = split_weights(w_gate, w_up, w_down)

    def expert_bwd(operands):
        in_rows, grad_rows, gate_w, up_w, down_w = operands
        back_gate = jnp.dot(in_rows, gate_w, preferred_element_type=jnp.float32)
        back_up = jnp.dot(in_rows, up_w, preferred_element_type=jnp.float32)
        back_hid = jnp.dot(grad_rows, down_w.T, preferred_element_type=jnp.float32)
        sigmoid_g = jax.nn.sigmoid(back_gate)
        grad_gate = (back_hid * back_up * sigmoid_g * (1.0 + back_gate * (1.0 - sigmoid_g))).astype(jnp.bfloat16)
        grad_up = (back_hid * back_gate * sigmoid_g).astype(jnp.bfloat16)
        grad_gate = grad_gate.reshape(-1, GROUP, HDEV).astype(jnp.float32)
        grad_up = grad_up.reshape(-1, GROUP, HDEV).astype(jnp.float32)
        gate_q = gate_w.reshape(D, GROUP, HDEV).astype(jnp.float32)
        up_q = up_w.reshape(D, GROUP, HDEV).astype(jnp.float32)
        quarters = jnp.einsum("mgh,dgh->gmd", grad_gate, gate_q) + jnp.einsum("mgh,dgh->gmd", grad_up, up_q)
        return jnp.sum(quarters.astype(jnp.bfloat16).astype(jnp.float32), axis=0)

    outputs = lax.map(expert_bwd, (in_buffer, grad_buffer, gate_e, up_e, down_e)).reshape(-1, D)
    branch = outputs[dest_rows]
    return (grads.astype(jnp.float32) + gate_prob[:, None] * branch).astype(jnp.bfloat16)


def reference(forward_in, forward_route, forward_gate_prob, backward_in, backward_route, backward_gate_prob, cotangent, w_gate, w_up, w_down):
    forward_out = lax.map(lambda operands: forward_segment(*operands), (forward_in, forward_route[:, :, 0], forward_gate_prob[:, :, 0], w_gate, w_up, w_down))
    backward_out = lax.map(lambda operands: backward_segment(*operands), (backward_in, backward_route[:, :, 0], backward_gate_prob[:, :, 0], cotangent, w_gate, w_up, w_down))
    return jnp.roll(forward_out, 1, axis=0), jnp.roll(backward_out, -1, axis=0)
```

```python
import functools

import jax
import jax.numpy as jnp
from jax import lax
from jax.experimental import pallas as pl
from jax.experimental.pallas import tpu as pltpu
from jax.sharding import PartitionSpec as P

MESH = pl.DeviceIdType.MESH
F32 = jnp.float32
BF16 = jnp.bfloat16

GROUP = 4
SLOTS = 16
EXTRA = 4
CHUNKS = 4


def dot(left, right):
    return jnp.dot(left, right, preferred_element_type=F32)


def dot_last(left, right):
    return lax.dot_general(left, right, (((1,), (1,)), ((), ())), preferred_element_type=F32)


def iota(shape, dim):
    return lax.broadcasted_iota(jnp.int32, shape, dim)


def multiple(value, of):
    return pl.multiple_of(value, of)


def kernel(
    experts,
    pipes,
    fwd_in,
    bwd_in,
    cot_in,
    w_gate,
    w_up,
    w_down,
    fwd_route,
    bwd_route,
    fwd_prob,
    bwd_prob,
    next_fwd,
    next_cot,
    rows_in,
    packed,
    tokens,
    gate,
    up,
    down,
    stack,
    acc,
    hidden,
    grads,
    mine,
    theirs,
    others,
    summed,
    back,
    final,
    sel_in,
    sel_out,
    unfold,
    fold,
    local_sem,
    w_send,
    w_recv,
    d_send,
    d_recv,
    t_send,
    t_recv,
    c_send,
    c_recv,
    r_send,
    r_recv,
    p_send,
    p_recv,
):
    tok, width = rows_in.shape[1], rows_in.shape[2]
    part = width // CHUNKS
    quarter = part // EXTRA
    hdev = gate.shape[2]
    main = experts * SLOTS

    section = lax.axis_index("pipe")
    member = lax.axis_index("expert")
    core = section % 2
    x = member % GROUP
    me = member // GROUP
    pair_a = x + 1 - 2 * (x % 2)
    pair_b = GROUP - 1 - x
    token_mate = (section, me * GROUP + (1 - core) * pair_a + core * pair_b)
    weight_mate = (section, me * GROUP + core * pair_a + (1 - core) * pair_b)
    upstream = ((section + 1) % pipes, member)
    downstream = ((section + pipes - 1) % pipes, member)

    def peer(k):
        return (me + k) % experts

    def remote(src, dst, send, recv, device):
        return pltpu.make_async_remote_copy(
            src_ref=src, dst_ref=dst, send_sem=send, recv_sem=recv, device_id=device, device_id_type=MESH
        )

    def cols(c):
        return pl.ds(multiple(c * part, part), part)

    def weight_copy(i, c):
        if i < 2:
            src, dst = ((w_gate, gate), (w_up, up))[i]
            return remote(
                src.at[0, cols(c)], dst.at[1, cols(c)], w_send.at[i, c], w_recv.at[i, c], weight_mate
            )
        return remote(
            w_down.at[0, :, cols(c)],
            down.at[c, pl.ds(hdev, hdev)],
            w_send.at[i, c],
            w_recv.at[i, c],
            weight_mate,
        )

    def slot_rows(k):
        return pl.ds(multiple(k * SLOTS, SLOTS), SLOTS)

    def spread_copy(src, dst, send, recv, i, c, k):
        to = peer(k)
        return remote(
            src.at[i, c, slot_rows(to)],
            dst.at[i, c, slot_rows(me)],
            send.at[i, c, k],
            recv.at[i, c, k],
            (section, to * GROUP + x),
        )

    def dispatch(i, c, k):
        return spread_copy(packed, tokens, d_send, d_recv, i, c, k)

    def give_back(i, c, k):
        return spread_copy(summed, back, r_send, r_recv, i, c, k)

    def mate_copy(i, c):
        return remote(
            tokens.at[i, c, pl.ds(0, main)],
            tokens.at[i, c, pl.ds(main, main)],
            t_send.at[i, c],
            t_recv.at[i, c],
            token_mate,
        )

    def result_copy(i, c):
        return remote(theirs.at[i, c], others.at[i, c], c_send.at[i, c], c_recv.at[i, c], token_mate)

    def relay_copy(i, c):
        out = (next_fwd, next_cot)[i]
        return remote(
            final.at[i, c],
            out.at[0, :, cols(c)],
            p_send.at[i, c],
            p_recv.at[i, c],
            (upstream, downstream)[i],
        )

    def each(body, count=CHUNKS):
        lax.fori_loop(0, count, lambda c, carry: (body(c), carry)[1], 0)

    local = [
        pltpu.make_async_copy(src.at[0], rows_in.at[i], local_sem.at[i])
        for i, src in enumerate((fwd_in, bwd_in, cot_in))
    ]
    local.append(pltpu.make_async_copy(w_gate.at[0], gate.at[0], local_sem.at[3]))
    local.append(pltpu.make_async_copy(w_up.at[0], up.at[0], local_sem.at[4]))
    for c in range(CHUNKS):
        local.append(
            pltpu.make_async_copy(
                w_down.at[0, :, pl.ds(c * part, part)], down.at[c, pl.ds(0, hdev)], local_sem.at[5 + c]
            )
        )
    for copy in local:
        copy.start()

    barrier = pltpu.get_barrier_semaphore()
    greeted = [(section, peer(k) * GROUP + x) for k in range(1, experts)]
    greeted += [token_mate, weight_mate, upstream, downstream]
    for device in greeted:
        pl.semaphore_signal(barrier, inc=1, device_id=device, device_id_type=MESH)

    def select(o, route):
        ids = route[0]
        lane = iota((tok, main), 1)
        token = iota((tok, main), 0)
        onehot = (lane == ids).astype(F32).astype(BF16)
        earlier = (lane < token).astype(F32).astype(BF16)
        before = dot(earlier, onehot)
        place = jnp.sum(before * onehot.astype(F32), axis=1, keepdims=True)
        lane_f = lane.astype(F32)
        first = ids.astype(F32) * SLOTS
        whole = jnp.where(place < SLOTS, first + place, -1.0)
        chosen = (whole == lane_f).astype(F32)
        sel_in[o, 0] = chosen.T.astype(BF16)
        for q in range(EXTRA):
            sel_out[o, q, :, 0:main] = chosen.astype(BF16)
        for q in range(EXTRA):
            folded = jnp.where(place >= SLOTS, first + (place - SLOTS) + q * EXTRA, -1.0)
            chosen = (folded == lane_f).astype(F32)
            sel_in[o, 1 + q] = chosen.T.astype(BF16)
            sel_out[o, q, :, main : 2 * main] = chosen.astype(BF16)

    select(0, fwd_route)
    select(1, bwd_route)

    extra = experts * EXTRA
    for q in range(EXTRA):
        r = iota((2 * extra, 2 * main), 0)
        i = iota((2 * extra, 2 * main), 1)
        unfold[q] = (i == (r // EXTRA) * SLOTS + q * EXTRA + r % EXTRA).astype(F32).astype(BF16)
        r = iota((2 * main, 2 * extra), 1)
        i = iota((2 * main, 2 * extra), 0)
        fold[q] = (i == (r // EXTRA) * SLOTS + q * EXTRA + r % EXTRA).astype(F32).astype(BF16)
    acc[...] = jnp.zeros_like(acc)

    pl.semaphore_wait(barrier, len(greeted))
    for i in range(3):
        each(lambda c: weight_copy(i, c).start())

    for i in range(3):
        o = min(i, 1)
        local[i].wait()

        def pack(c, i=i, o=o):
            rows = rows_in[i, :, cols(c)]
            packed[i, c, :, 0:part] = dot(sel_in[o, 0], rows).astype(BF16)
            total = dot(sel_in[o, 1], rows[:, 0:quarter])
            for q in range(1, EXTRA):
                total += dot(sel_in[o, 1 + q], rows[:, q * quarter : (q + 1) * quarter])
            packed[i, c, :, part:] = total.astype(BF16)
            for k in range(1, experts):
                dispatch(i, c, k).start()
            tokens[i, c, slot_rows(me)] = packed[i, c, slot_rows(me)]

        each(pack)

    for i in range(3):

        def pass_on(c, i=i):
            for k in range(1, experts):
                dispatch(i, c, k).wait_recv()
            mate_copy(i, c).start()

        each(pass_on)

    for copy in local[3:]:
        copy.wait()

    def load(i, c):
        stack[0 : 2 * main] = tokens[i, c, :, 0:part]
        folded = tokens[i, c, :, part:]
        for q in range(EXTRA):
            stack[2 * main :, q * quarter : (q + 1) * quarter] = dot(unfold[q], folded).astype(BF16)

    def store(o, c, value):
        mine[o, c, :, 0:part] = value[0:main].astype(BF16)
        theirs[o, c, :, 0:part] = value[main : 2 * main].astype(BF16)
        rest = value[2 * main :].astype(BF16)
        total = dot(fold[0], rest[:, 0:quarter])
        for q in range(1, EXTRA):
            total += dot(fold[q], rest[:, q * quarter : (q + 1) * quarter])
        mine[o, c, :, part:] = total[0:main].astype(BF16)
        theirs[o, c, :, part:] = total[main:].astype(BF16)
        result_copy(o, c).start()

    def project(i, c):
        load(i, c)
        for half in range(2):
            at = pl.ds(half * hdev, hdev)
            acc[2 * i, :, at] += dot(stack[...], gate[half, cols(c)])
            acc[2 * i + 1, :, at] += dot(stack[...], up[half, cols(c)])

    def forward_in_step(c):
        mate_copy(0, c).wait_recv()
        weight_copy(0, c).wait_recv()
        weight_copy(1, c).wait_recv()
        project(0, c)

    each(forward_in_step)
    gate_pre = acc[0]
    hidden[...] = (gate_pre / (1.0 + jnp.exp(-gate_pre)) * acc[1]).astype(BF16)

    def backward_in_step(c):
        mate_copy(1, c).wait_recv()
        project(1, c)

    each(backward_in_step)

    def down_step(c):
        weight_copy(2, c).wait_recv()
        store(0, c, dot(hidden[...], down[c]))
        mate_copy(2, c).wait_recv()
        load(2, c)
        acc[4] += dot_last(stack[...], down[c])

    each(down_step)

    back_gate = acc[2]
    back_hid = acc[4]
    g = 1.0 / (1.0 + jnp.exp(-back_gate))
    grads[0] = (back_hid * acc[3] * g * (1.0 + back_gate * (1.0 - g))).astype(BF16)
    grads[1] = (back_hid * back_gate * g).astype(BF16)

    def return_step(o, c):
        result_copy(o, c).wait_recv()
        summed[o, c] = (mine[o, c].astype(F32) + others[o, c].astype(F32)).astype(BF16)
        for k in range(1, experts):
            give_back(o, c, k).start()
        back[o, c, slot_rows(me)] = summed[o, c, slot_rows(me)]

    def backward_step(c):
        total = dot_last(grads[0, :, 0:hdev], gate[0, cols(c)])
        total += dot_last(grads[0, :, hdev:], gate[1, cols(c)])
        total += dot_last(grads[1, :, 0:hdev], up[0, cols(c)])
        total += dot_last(grads[1, :, hdev:], up[1, cols(c)])
        store(1, c, total)
        return_step(0, c)

    each(backward_step)

    def finish(o, c):
        for k in range(1, experts):
            give_back(o, c, k).wait_recv()
        prob = (fwd_prob, bwd_prob)[o][0]
        res = 2 * o
        for q in range(EXTRA):
            at = pl.ds(multiple(c * part + q * quarter, quarter), quarter)
            branch = dot(sel_out[o, q, :, 0:main], back[o, c, :, q * quarter : (q + 1) * quarter])
            branch += dot(sel_out[o, q, :, main:], back[o, c, :, part:])
            value = rows_in[res, :, at].astype(F32) + prob * branch
            final[o, c, :, q * quarter : (q + 1) * quarter] = value.astype(BF16)
        relay_copy(o, c).start()

    def end_step(c):
        finish(0, c)
        return_step(1, c)

    each(end_step)
    each(lambda c: finish(1, c))

    def drain(c):
        for i in range(3):
            weight_copy(i, c).wait_send()
            mate_copy(i, c).wait_send()
            for k in range(1, experts):
                dispatch(i, c, k).wait_send()
        for o in range(2):
            result_copy(o, c).wait_send()
            for k in range(1, experts):
                give_back(o, c, k).wait_send()
            relay_copy(o, c).wait()

    each(drain)


def on_device(
    forward_in,
    forward_route,
    forward_gate_prob,
    backward_in,
    backward_route,
    backward_gate_prob,
    cotangent,
    w_gate,
    w_up,
    w_down,
):
    experts = lax.axis_size("expert") // GROUP
    pipes = lax.axis_size("pipe")
    _, tok, width = forward_in.shape
    hdev = w_gate.shape[2]
    main = experts * SLOTS
    extra = experts * EXTRA
    part = width // CHUNKS
    wide = part + part // EXTRA
    rows = 2 * (main + extra)
    hbm = pl.BlockSpec(memory_space=pl.ANY)
    vmem = pl.BlockSpec(memory_space=pltpu.VMEM)
    dma = pltpu.SemaphoreType.DMA
    return pl.pallas_call(
        functools.partial(kernel, experts, pipes),
        out_shape=[jax.ShapeDtypeStruct(forward_in.shape, BF16)] * 2,
        in_specs=[hbm] * 6 + [vmem] * 4,
        out_specs=[hbm] * 2,
        scratch_shapes=[
            pltpu.VMEM((3, tok, width), BF16),
            pltpu.VMEM((3, CHUNKS, main, wide), BF16),
            pltpu.VMEM((3, CHUNKS, 2 * main, wide), BF16),
            pltpu.VMEM((2, width, hdev), BF16),
            pltpu.VMEM((2, width, hdev), BF16),
            pltpu.VMEM((CHUNKS, 2 * hdev, part), BF16),
            pltpu.VMEM((rows, part), BF16),
            pltpu.VMEM((5, rows, 2 * hdev), F32),
            pltpu.VMEM((rows, 2 * hdev), BF16),
            pltpu.VMEM((2, rows, 2 * hdev), BF16),
            pltpu.VMEM((2, CHUNKS, main, wide), BF16),
            pltpu.VMEM((2, CHUNKS, main, wide), BF16),
            pltpu.VMEM((2, CHUNKS, main, wide), BF16),
            pltpu.VMEM((2, CHUNKS, main, wide), BF16),
            pltpu.VMEM((2, CHUNKS, main, wide), BF16),
            pltpu.VMEM((2, CHUNKS, tok, part), BF16),
            pltpu.VMEM((2, 1 + EXTRA, main, tok), BF16),
            pltpu.VMEM((2, EXTRA, tok, 2 * main), BF16),
            pltpu.VMEM((EXTRA, 2 * extra, 2 * main), BF16),
            pltpu.VMEM((EXTRA, 2 * main, 2 * extra), BF16),
            dma((5 + CHUNKS,)),
            dma((3, CHUNKS)),
            dma((3, CHUNKS)),
            dma((3, CHUNKS, experts)),
            dma((3, CHUNKS, experts)),
            dma((3, CHUNKS)),
            dma((3, CHUNKS)),
            dma((2, CHUNKS)),
            dma((2, CHUNKS)),
            dma((2, CHUNKS, experts)),
            dma((2, CHUNKS, experts)),
            dma((2, CHUNKS)),
            dma((2, CHUNKS)),
        ],
        compiler_params=pltpu.CompilerParams(
            collective_id=1, has_side_effects=True, vmem_limit_bytes=60 * 2**20
        ),
    )(
        forward_in,
        backward_in,
        cotangent,
        w_gate,
        w_up,
        w_down,
        forward_route,
        backward_route,
        forward_gate_prob,
        backward_gate_prob,
    )


def solution(mesh):
    tokens = P("pipe", "expert", None)
    columns = P("pipe", None, "expert")
    return jax.shard_map(
        lambda *args: tuple(on_device(*args)),
        mesh=mesh,
        in_specs=(tokens,) * 7 + (columns, columns, tokens),
        out_specs=(tokens, tokens),
        check_vma=False,
    )
```

```python
import functools

import jax
import jax.numpy as jnp
from jax import lax
from jax.experimental import pallas as pl
from jax.experimental.pallas import tpu as pltpu
from jax.sharding import PartitionSpec as P

MESH = pl.DeviceIdType.MESH
F32 = jnp.float32
BF16 = jnp.bfloat16

GROUP = 4
SLOTS = 16
EXTRA = 4
CHUNKS = 4
SETS = 2


def dot(left, right):
    return jnp.dot(left, right, preferred_element_type=F32)


def dot_last(left, right):
    return lax.dot_general(left, right, (((1,), (1,)), ((), ())), preferred_element_type=F32)


def iota(shape, dim):
    return lax.broadcasted_iota(jnp.int32, shape, dim)


def multiple(value, of):
    return pl.multiple_of(value, of)


def kernel(
    experts,
    pipes,
    fwd_in,
    bwd_in,
    cot_in,
    w_gate,
    w_up,
    w_down,
    fwd_route,
    bwd_route,
    fwd_prob,
    bwd_prob,
    next_fwd,
    next_cot,
    rows_in,
    packed,
    tokens,
    gate,
    up,
    down,
    stack,
    acc,
    hidden,
    grads,
    mine,
    theirs,
    others,
    summed,
    back,
    resid,
    far_route,
    far_prob,
    prob,
    final,
    sel_in,
    sel_out,
    unfold,
    fold,
    local_sem,
    w_send,
    w_recv,
    d_send,
    d_recv,
    t_send,
    t_recv,
    c_send,
    c_recv,
    r_send,
    r_recv,
    m_send,
    m_recv,
    out_sem,
):
    tok, width = rows_in.shape[1], rows_in.shape[2]
    part = width // CHUNKS
    quarter = part // EXTRA
    hdev = gate.shape[2]
    main = experts * SLOTS
    members = experts // SETS
    block = members * SLOTS

    section = lax.axis_index("pipe")
    member = lax.axis_index("expert")
    core = section % 2
    x = member % GROUP
    me = member // GROUP
    pair_a = x + 1 - 2 * (x % 2)
    pair_b = GROUP - 1 - x
    token_mate = (section, me * GROUP + (1 - core) * pair_a + core * pair_b)
    weight_mate = (section, me * GROUP + core * pair_a + (1 - core) * pair_b)
    ahead = (section + 1) % pipes
    behind = (section + pipes - 1) % pipes

    def peer(k):
        return (me + k) % experts

    def set_of(j):
        return (j // 4 + j) % SETS

    def place_of(j):
        return j // SETS

    def source(s, place):
        z = (place * SETS) // 4
        return place * SETS + (s + z) % SETS

    def remote(src, dst, send, recv, device):
        return pltpu.make_async_remote_copy(
            src_ref=src, dst_ref=dst, send_sem=send, recv_sem=recv, device_id=device, device_id_type=MESH
        )

    def cols(c):
        return pl.ds(multiple(c * part, part), part)

    def slot_rows(k):
        return pl.ds(multiple(k * SLOTS, SLOTS), SLOTS)

    def weight_copy(i, c):
        if i < 2:
            held = (gate, up)[i]
            return remote(
                held.at[0, cols(c)], held.at[1, cols(c)], w_send.at[i, c], w_recv.at[i, c], weight_mate
            )
        return remote(
            down.at[c, pl.ds(0, hdev)],
            down.at[c, pl.ds(hdev, hdev)],
            w_send.at[i, c],
            w_recv.at[i, c],
            weight_mate,
        )

    def dispatch(i, c, k):
        to = peer(k)
        return remote(
            packed.at[i, c, slot_rows(to)],
            tokens.at[i, set_of(me), c, slot_rows(place_of(me))],
            d_send.at[i, c, k],
            d_recv.at[i, c, me],
            (section, to * GROUP + x),
        )

    def dispatch_from(i, c, j):
        return remote(
            packed.at[i, c, slot_rows(j)],
            tokens.at[i, set_of(j), c, slot_rows(place_of(j))],
            d_send.at[i, c, 0],
            d_recv.at[i, c, j],
            (section, j * GROUP + x),
        )

    def mate_copy(i, s, c):
        return remote(
            tokens.at[i, s, c, pl.ds(0, block)],
            tokens.at[i, s, c, pl.ds(block, block)],
            t_send.at[i, s, c],
            t_recv.at[i, s, c],
            token_mate,
        )

    def result_copy(o, s, c):
        return remote(
            theirs.at[o, s, c], others.at[o, s, c], c_send.at[o, s, c], c_recv.at[o, s, c], token_mate
        )

    def give(o, s, c, place):
        j = source(s, place)
        return remote(
            summed.at[o, s, c, slot_rows(place)],
            back.at[o, c, slot_rows(me)],
            r_send.at[o, c, j],
            r_recv.at[o, c, me],
            ((ahead, behind)[o], j * GROUP + x),
        )

    def give_from(o, c, j):
        return remote(
            summed.at[o, 0, c, slot_rows(0)],
            back.at[o, c, slot_rows(j)],
            r_send.at[o, c, j],
            r_recv.at[o, c, j],
            ((ahead, behind)[o], j * GROUP + x),
        )

    def message(i, o):
        src, dst = (
            ((fwd_in, cot_in)[o].at[0], resid.at[o]),
            ((fwd_route, bwd_route)[o], far_route.at[o]),
            ((fwd_prob, bwd_prob)[o], far_prob.at[o]),
        )[i]
        return remote(src, dst, m_send.at[i, o], m_recv.at[i, o], ((ahead, behind)[o], member))

    def out_copy(o, c):
        out = (next_fwd, next_cot)[o]
        return pltpu.make_async_copy(final.at[o, c], out.at[0, :, cols(c)], out_sem.at[o, c])

    def each(body, count=CHUNKS):
        lax.fori_loop(0, count, lambda c, carry: (body(c), carry)[1], 0)

    local = [
        pltpu.make_async_copy(src.at[0], rows_in.at[i], local_sem.at[i])
        for i, src in enumerate((fwd_in, bwd_in, cot_in))
    ]
    local.append(pltpu.make_async_copy(w_gate.at[0], gate.at[0], local_sem.at[3]))
    local.append(pltpu.make_async_copy(w_up.at[0], up.at[0], local_sem.at[4]))
    for c in range(CHUNKS):
        local.append(
            pltpu.make_async_copy(
                w_down.at[0, :, pl.ds(c * part, part)], down.at[c, pl.ds(0, hdev)], local_sem.at[5 + c]
            )
        )
    for copy in local[3:5] + local[:3] + local[5:]:
        copy.start()

    barrier = pltpu.get_barrier_semaphore()

    def greet(device):
        pl.semaphore_signal(barrier, inc=1, device_id=device, device_id_type=MESH)

    greet(token_mate)
    greet(weight_mate)
    each(lambda k: greet((section, peer(k + 1) * GROUP + x)), experts - 1)
    each(lambda k: greet((ahead, k * GROUP + x)), experts)
    each(lambda k: greet((behind, k * GROUP + x)), experts)

    pl.semaphore_wait(barrier, 2 + (experts - 1) + 2 * experts)
    for i in range(3):
        for copy in (local[3:4], local[4:5], local[5:])[i]:
            copy.wait()
        each(lambda c: weight_copy(i, c).start())

    def slots_of(route):
        onehot = (iota((SLOTS, tok), 0) == route).astype(F32)
        earlier = (iota((tok, tok), 0) < iota((tok, tok), 1)).astype(F32).astype(BF16)
        before = dot(onehot.astype(BF16), earlier)
        place = jnp.sum(before * onehot, axis=0, keepdims=True)
        return route.astype(F32) * SLOTS, place

    def chosen(first, place, q):
        if q < 0:
            slot = jnp.where(place < SLOTS, first + place, -1.0)
        else:
            slot = jnp.where(place >= SLOTS, first + (place - SLOTS) + q * EXTRA, -1.0)
        return (slot == iota((main, tok), 0).astype(F32)).astype(F32)

    for o in range(2):
        first, place = slots_of((fwd_route, bwd_route)[o][...])
        for q in range(1 + EXTRA):
            sel_in[o, q] = chosen(first, place, q - 1).astype(BF16)

    for o in range(2):
        message(1, o).start()
        message(2, o).start()

    for i in range(3):
        o = min(i, 1)
        local[i].wait()

        def pack(c, i=i, o=o):
            rows = rows_in[i, :, cols(c)]
            packed[i, c, :, 0:part] = dot(sel_in[o, 0], rows).astype(BF16)
            total = dot(sel_in[o, 1], rows[:, 0:quarter])
            for q in range(1, EXTRA):
                total += dot(sel_in[o, 1 + q], rows[:, q * quarter : (q + 1) * quarter])
            packed[i, c, :, part:] = total.astype(BF16)
            for k in range(1, experts):
                dispatch(i, c, k).start()
            tokens[i, set_of(me), c, slot_rows(place_of(me))] = packed[i, c, slot_rows(me)]

        each(pack)

    for o in range(2):
        message(0, o).start()

    def pass_on(i, s, c):
        for place in range(members):
            j = source(s, place)

            @pl.when(j != me)
            def _():
                dispatch_from(i, c, j).wait_recv()

        mate_copy(i, s, c).start()

    for i in range(3):
        each(lambda c: pass_on(i, 0, c))

    extra = members * EXTRA
    for q in range(EXTRA):
        r = iota((2 * extra, 2 * block), 0)
        i = iota((2 * extra, 2 * block), 1)
        unfold[q] = (i == (r // EXTRA) * SLOTS + q * EXTRA + r % EXTRA).astype(F32).astype(BF16)
        r = iota((2 * block, 2 * extra), 1)
        i = iota((2 * block, 2 * extra), 0)
        fold[q] = (i == (r // EXTRA) * SLOTS + q * EXTRA + r % EXTRA).astype(F32).astype(BF16)

    for o in range(2):
        message(1, o).wait_recv()
        message(2, o).wait_recv()
        first, place = slots_of(far_route[o])
        whole = chosen(first, place, -1).T.astype(BF16)
        for q in range(EXTRA):
            sel_out[o, q, :, 0:main] = whole
            sel_out[o, q, :, main : 2 * main] = chosen(first, place, q).T.astype(BF16)
        prob[o] = jnp.broadcast_to(far_prob[o], (tok, tok)).T

    def load(i, s, c):
        stack[0 : 2 * block] = tokens[i, s, c, :, 0:part]
        folded = tokens[i, s, c, :, part:]
        for q in range(EXTRA):
            stack[2 * block :, q * quarter : (q + 1) * quarter] = dot(unfold[q], folded).astype(BF16)

    def store(o, s, c, value):
        mine[o, s, c, :, 0:part] = value[0:block].astype(BF16)
        theirs[o, s, c, :, 0:part] = value[block : 2 * block].astype(BF16)
        rest = value[2 * block :].astype(BF16)
        total = dot(fold[0], rest[:, 0:quarter])
        for q in range(1, EXTRA):
            total += dot(fold[q], rest[:, q * quarter : (q + 1) * quarter])
        mine[o, s, c, :, part:] = total[0:block].astype(BF16)
        theirs[o, s, c, :, part:] = total[block:].astype(BF16)
        result_copy(o, s, c).start()

    def project(i, s, c):
        load(i, s, c)
        for half in range(2):
            at = pl.ds(half * hdev, hdev)
            acc[2 * i, :, at] += dot(stack[...], gate[half, cols(c)])
            acc[2 * i + 1, :, at] += dot(stack[...], up[half, cols(c)])

    def first_part(s):
        acc[...] = jnp.zeros_like(acc)

        def forward_in_step(c):
            mate_copy(0, s, c).wait_recv()
            if s == 0:
                weight_copy(0, c).wait_recv()
                weight_copy(1, c).wait_recv()
            project(0, s, c)

        def backward_in_step(c):
            mate_copy(1, s, c).wait_recv()
            project(1, s, c)

        def down_step(c):
            if s == 0:
                weight_copy(2, c).wait_recv()
            store(0, s, c, dot(hidden[...], down[c]))

        def cot_step(c):
            mate_copy(2, s, c).wait_recv()
            load(2, s, c)
            acc[4] += dot_last(stack[...], down[c])

        def both_steps(c):
            down_step(c)
            cot_step(c)

        each(forward_in_step)
        gate_pre = acc[0]
        hidden[...] = (gate_pre / (1.0 + jnp.exp(-gate_pre)) * acc[1]).astype(BF16)
        if s == 0:
            each(backward_in_step)
            each(both_steps)
        else:
            each(down_step)
            each(backward_in_step)
            each(cot_step)

    def second_part(s, beside):
        back_gate = acc[2]
        back_hid = acc[4]
        g = 1.0 / (1.0 + jnp.exp(-back_gate))
        grads[0] = (back_hid * acc[3] * g * (1.0 + back_gate * (1.0 - g))).astype(BF16)
        grads[1] = (back_hid * back_gate * g).astype(BF16)

        def backward_step(c):
            total = dot_last(grads[0, :, 0:hdev], gate[0, cols(c)])
            total += dot_last(grads[0, :, hdev:], gate[1, cols(c)])
            total += dot_last(grads[1, :, 0:hdev], up[0, cols(c)])
            total += dot_last(grads[1, :, hdev:], up[1, cols(c)])
            store(1, s, c, total)
            beside(c)

        each(backward_step)

    def return_step(o, s, c):
        result_copy(o, s, c).wait_recv()
        summed[o, s, c] = (mine[o, s, c].astype(F32) + others[o, s, c].astype(F32)).astype(BF16)
        for place in range(members):
            give(o, s, c, place).start()

    def finish(o, c):
        for j in range(experts):
            give_from(o, c, j).wait_recv()
        scale = jnp.concatenate([prob[o]] * (quarter // tok), axis=1)
        for q in range(EXTRA):
            at = pl.ds(multiple(c * part + q * quarter, quarter), quarter)
            branch = dot(sel_out[o, q, :, 0:main], back[o, c, :, q * quarter : (q + 1) * quarter])
            branch += dot(sel_out[o, q, :, main:], back[o, c, :, part:])
            value = resid[o, :, at].astype(F32) + scale * branch
            final[o, c, :, q * quarter : (q + 1) * quarter] = value.astype(BF16)
        out_copy(o, c).start()

    for s in range(SETS):
        first_part(s)
        if s + 1 < SETS:
            each(lambda c: pass_on(0, s + 1, c))
            second_part(s, lambda c: None)
            for i in range(1, 3):
                each(lambda c: pass_on(i, s + 1, c))
            each(lambda c: return_step(0, s, c))
            each(lambda c: return_step(1, s, c))
        else:
            second_part(s, lambda c: return_step(0, s, c))
            each(lambda c: return_step(1, s, c))

    for o in range(2):
        message(0, o).wait_recv()
    each(lambda c: finish(0, c))
    each(lambda c: finish(1, c))

    def drain(c):
        for i in range(3):
            weight_copy(i, c).wait_send()
            for s in range(SETS):
                mate_copy(i, s, c).wait_send()
            for k in range(1, experts):
                dispatch(i, c, k).wait_send()
        for o in range(2):
            for s in range(SETS):
                result_copy(o, s, c).wait_send()
                for place in range(members):
                    give(o, s, c, place).wait_send()
            out_copy(o, c).wait()

    each(drain)
    for i in range(3):
        for o in range(2):
            message(i, o).wait_send()


def on_device(
    forward_in,
    forward_route,
    forward_gate_prob,
    backward_in,
    backward_route,
    backward_gate_prob,
    cotangent,
    w_gate,
    w_up,
    w_down,
):
    experts = lax.axis_size("expert") // GROUP
    pipes = lax.axis_size("pipe")
    _, tok, width = forward_in.shape
    hdev = w_gate.shape[2]
    main = experts * SLOTS
    members = experts // SETS
    block = members * SLOTS
    extra = members * EXTRA
    part = width // CHUNKS
    wide = part + part // EXTRA
    rows = 2 * (block + extra)
    hbm = pl.BlockSpec(memory_space=pl.ANY)
    vmem = pl.BlockSpec(memory_space=pltpu.VMEM)
    dma = pltpu.SemaphoreType.DMA
    return pl.pallas_call(
        functools.partial(kernel, experts, pipes),
        out_shape=[jax.ShapeDtypeStruct(forward_in.shape, BF16)] * 2,
        in_specs=[hbm] * 6 + [vmem] * 4,
        out_specs=[hbm] * 2,
        scratch_shapes=[
            pltpu.VMEM((3, tok, width), BF16),
            pltpu.VMEM((3, CHUNKS, main, wide), BF16),
            pltpu.VMEM((3, SETS, CHUNKS, 2 * block, wide), BF16),
            pltpu.VMEM((2, width, hdev), BF16),
            pltpu.VMEM((2, width, hdev), BF16),
            pltpu.VMEM((CHUNKS, 2 * hdev, part), BF16),
            pltpu.VMEM((rows, part), BF16),
            pltpu.VMEM((5, rows, 2 * hdev), F32),
            pltpu.VMEM((rows, 2 * hdev), BF16),
            pltpu.VMEM((2, rows, 2 * hdev), BF16),
            pltpu.VMEM((2, SETS, CHUNKS, block, wide), BF16),
            pltpu.VMEM((2, SETS, CHUNKS, block, wide), BF16),
            pltpu.VMEM((2, SETS, CHUNKS, block, wide), BF16),
            pltpu.VMEM((2, SETS, CHUNKS, block, wide), BF16),
            pltpu.VMEM((2, CHUNKS, main, wide), BF16),
            pltpu.VMEM((2, tok, width), BF16),
            pltpu.VMEM((2, 1, tok), jnp.int32),
            pltpu.VMEM((2, 1, tok), F32),
            pltpu.VMEM((2, tok, tok), F32),
            pltpu.VMEM((2, CHUNKS, tok, part), BF16),
            pltpu.VMEM((2, 1 + EXTRA, main, tok), BF16),
            pltpu.VMEM((2, EXTRA, tok, 2 * main), BF16),
            pltpu.VMEM((EXTRA, 2 * extra, 2 * block), BF16),
            pltpu.VMEM((EXTRA, 2 * block, 2 * extra), BF16),
            dma((5 + CHUNKS,)),
            dma((3, CHUNKS)),
            dma((3, CHUNKS)),
            dma((3, CHUNKS, experts)),
            dma((3, CHUNKS, experts)),
            dma((3, SETS, CHUNKS)),
            dma((3, SETS, CHUNKS)),
            dma((2, SETS, CHUNKS)),
            dma((2, SETS, CHUNKS)),
            dma((2, CHUNKS, experts)),
            dma((2, CHUNKS, experts)),
            dma((3, 2)),
            dma((3, 2)),
            dma((2, CHUNKS)),
        ],
        compiler_params=pltpu.CompilerParams(
            collective_id=1, has_side_effects=True, vmem_limit_bytes=60 * 2**20
        ),
    )(
        forward_in,
        backward_in,
        cotangent,
        w_gate,
        w_up,
        w_down,
        forward_route.reshape(1, tok),
        backward_route.reshape(1, tok),
        forward_gate_prob.reshape(1, tok),
        backward_gate_prob.reshape(1, tok),
    )


def solution(mesh):
    tokens = P("pipe", "expert", None)
    columns = P("pipe", None, "expert")
    return jax.shard_map(
        lambda *args: tuple(on_device(*args)),
        mesh=mesh,
        in_specs=(tokens,) * 7 + (columns, columns, tokens),
        out_specs=(tokens, tokens),
        check_vma=False,
    )
```

```python
import functools

import jax
import jax.numpy as jnp
from jax import lax
from jax.experimental import pallas as pl
from jax.experimental.pallas import tpu as pltpu
from jax.sharding import PartitionSpec as P

MESH = pl.DeviceIdType.MESH
F32 = jnp.float32
BF16 = jnp.bfloat16

GROUP = 4
SLOTS = 16
EXTRA = 4
CHUNKS = 4
SPLIT = (8,)
SETS = len(SPLIT)
LATE = ((0, 1), (2, 2))
START = tuple(sum(SPLIT[:s]) for s in range(SETS))


def dot(left, right):
    return jnp.dot(left, right, preferred_element_type=F32)


def dot_last(left, right):
    return lax.dot_general(left, right, (((1,), (1,)), ((), ())), preferred_element_type=F32)


def iota(shape, dim):
    return lax.broadcasted_iota(jnp.int32, shape, dim)


def multiple(value, of):
    return pl.multiple_of(value, of)


def kernel(
    experts,
    pipes,
    fwd_in,
    bwd_in,
    cot_in,
    w_gate,
    w_up,
    w_down,
    fwd_route,
    bwd_route,
    fwd_prob,
    bwd_prob,
    next_fwd,
    next_cot,
    rows_in,
    packed,
    tokens,
    gate,
    up,
    down,
    stack,
    acc,
    hidden,
    grads,
    mine,
    theirs,
    others,
    summed,
    back,
    resid,
    far_route,
    far_prob,
    prob,
    final,
    sel_in,
    sel_out,
    unfold,
    fold,
    local_sem,
    w_send,
    w_recv,
    d_send,
    d_recv,
    t_send,
    t_recv,
    c_send,
    c_recv,
    r_send,
    r_recv,
    m_send,
    m_recv,
    out_sem,
):
    tok, width = rows_in.shape[1], rows_in.shape[2]
    part = width // CHUNKS
    quarter = part // EXTRA
    hdev = gate.shape[2]
    main = experts * SLOTS

    section = lax.axis_index("pipe")
    member = lax.axis_index("expert")
    core = section % 2
    x = member % GROUP
    me = member // GROUP
    pair_a = x + 1 - 2 * (x % 2)
    pair_b = GROUP - 1 - x
    token_mate = (section, me * GROUP + (1 - core) * pair_a + core * pair_b)
    weight_mate = (section, me * GROUP + core * pair_a + (1 - core) * pair_b)
    ahead = (section + 1) % pipes
    behind = (section + pipes - 1) % pipes

    def peer(k):
        return (me + k) % experts

    def rank_of(j):
        z = j // 4
        return (j + 2 * z + 3) % 4 * 2 + z

    def source(rank):
        z = rank % 2
        return z * 4 + (rank // 2 + 1 + 2 * z) % 4

    def own_row(rank):
        return rank + START[-1] * (rank // SPLIT[0])

    def remote(src, dst, send, recv, device):
        return pltpu.make_async_remote_copy(
            src_ref=src, dst_ref=dst, send_sem=send, recv_sem=recv, device_id=device, device_id_type=MESH
        )

    def cols(c):
        return pl.ds(multiple(c * part, part), part)

    def slot_rows(k):
        return pl.ds(multiple(k * SLOTS, SLOTS), SLOTS)

    def weight_copy(i, c):
        if i < 2:
            held = (gate, up)[i]
            return remote(
                held.at[0, cols(c)], held.at[1, cols(c)], w_send.at[i, c], w_recv.at[i, c], weight_mate
            )
        return remote(
            down.at[c, pl.ds(0, hdev)],
            down.at[c, pl.ds(hdev, hdev)],
            w_send.at[i, c],
            w_recv.at[i, c],
            weight_mate,
        )

    def set_rows(s, side=0, count=1):
        return pl.ds((2 * START[s] + side * SPLIT[s]) * SLOTS, count * SPLIT[s] * SLOTS)

    def part_rows(s):
        return pl.ds(START[s] * SLOTS, SPLIT[s] * SLOTS)

    def dispatch(i, c, k):
        to = peer(k)
        return remote(
            packed.at[i, c, slot_rows(to)],
            tokens.at[i, c, slot_rows(own_row(rank_of(me)))],
            d_send.at[i, c, k],
            d_recv.at[i, c, me],
            (section, to * GROUP + x),
        )

    def dispatch_from(i, c, rank):
        j = source(rank)
        return remote(
            packed.at[i, c, slot_rows(j)],
            tokens.at[i, c, slot_rows(own_row(rank))],
            d_send.at[i, c, 0],
            d_recv.at[i, c, j],
            (section, j * GROUP + x),
        )

    def mate_copy(i, s, c):
        return remote(
            tokens.at[i, c, set_rows(s)],
            tokens.at[i, c, set_rows(s, 1)],
            t_send.at[i, s, c],
            t_recv.at[i, s, c],
            token_mate,
        )

    def result_copy(o, s, c):
        return remote(
            theirs.at[o, c, part_rows(s)],
            others.at[o, c, part_rows(s)],
            c_send.at[o, s, c],
            c_recv.at[o, s, c],
            token_mate,
        )

    def give(o, c, rank):
        j = source(rank)
        return remote(
            summed.at[o, c, slot_rows(rank)],
            back.at[o, c, slot_rows(me)],
            r_send.at[o, c, j],
            r_recv.at[o, c, me],
            ((ahead, behind)[o], j * GROUP + x),
        )

    def give_from(o, c, j):
        return remote(
            summed.at[o, c, slot_rows(0)],
            back.at[o, c, slot_rows(j)],
            r_send.at[o, c, j],
            r_recv.at[o, c, j],
            ((ahead, behind)[o], j * GROUP + x),
        )

    def message(i, o):
        src, dst = (
            ((fwd_in, cot_in)[o].at[0], resid.at[o]),
            ((fwd_route, bwd_route)[o], far_route.at[o]),
            ((fwd_prob, bwd_prob)[o], far_prob.at[o]),
        )[i]
        return remote(src, dst, m_send.at[i, o], m_recv.at[i, o], ((ahead, behind)[o], member))

    def out_copy(o, c):
        out = (next_fwd, next_cot)[o]
        return pltpu.make_async_copy(final.at[o, c], out.at[0, :, cols(c)], out_sem.at[o, c])

    def each(body, count=CHUNKS):
        lax.fori_loop(0, count, lambda c, carry: (body(c), carry)[1], 0)

    local = [
        pltpu.make_async_copy(src.at[0], rows_in.at[i], local_sem.at[i])
        for i, src in enumerate((fwd_in, bwd_in, cot_in))
    ]
    local.append(pltpu.make_async_copy(w_gate.at[0], gate.at[0], local_sem.at[3]))
    local.append(pltpu.make_async_copy(w_up.at[0], up.at[0], local_sem.at[4]))
    for c in range(CHUNKS):
        local.append(
            pltpu.make_async_copy(
                w_down.at[0, :, pl.ds(c * part, part)], down.at[c, pl.ds(0, hdev)], local_sem.at[5 + c]
            )
        )
    for copy in local[3:5] + local[:3] + local[5:]:
        copy.start()

    barrier = pltpu.get_barrier_semaphore()

    def greet(device):
        pl.semaphore_signal(barrier, inc=1, device_id=device, device_id_type=MESH)

    greet(token_mate)
    greet(weight_mate)
    each(lambda k: greet((section, peer(k + 1) * GROUP + x)), experts - 1)
    each(lambda k: greet((ahead, k * GROUP + x)), experts)
    each(lambda k: greet((behind, k * GROUP + x)), experts)

    pl.semaphore_wait(barrier, 2 + (experts - 1) + 2 * experts)
    for i in range(3):
        for copy in (local[3:4], local[4:5], local[5:])[i]:
            copy.wait()
        each(lambda c: weight_copy(i, c).start())

    def slots_of(route):
        onehot = (iota((SLOTS, tok), 0) == route).astype(F32)
        earlier = (iota((tok, tok), 0) < iota((tok, tok), 1)).astype(F32).astype(BF16)
        before = dot(onehot.astype(BF16), earlier)
        place = jnp.sum(before * onehot, axis=0, keepdims=True)
        return route.astype(F32) * SLOTS, place

    def chosen(first, place, q):
        if q < 0:
            slot = jnp.where(place < SLOTS, first + place, -1.0)
        else:
            slot = jnp.where(place >= SLOTS, first + (place - SLOTS) + q * EXTRA, -1.0)
        return (slot == iota((main, tok), 0).astype(F32)).astype(F32)

    for o in range(2):
        first, place = slots_of((fwd_route, bwd_route)[o][...])
        for q in range(1 + EXTRA):
            sel_in[o, q] = chosen(first, place, q - 1).astype(BF16)

    for o in range(2):
        message(1, o).start()
        message(2, o).start()

    for copy in local[0:3]:
        copy.wait()

    def order(k):
        return (k + 1 - core) % 3

    def pack(n):
        i, c = order(n // CHUNKS), n % CHUNKS
        o = (i + 1) // 2
        rows = rows_in.at[i, :, cols(c)]
        packed[i, c, :, 0:part] = dot(sel_in[o, 0], rows[...]).astype(BF16)
        total = dot(sel_in[o, 1], rows[:, 0:quarter])
        for q in range(1, EXTRA):
            total += dot(sel_in[o, 1 + q], rows[:, q * quarter : (q + 1) * quarter])
        packed[i, c, :, part:] = total.astype(BF16)
        for k in range(1, experts):
            dispatch(i, c, k).start()
        tokens[i, c, slot_rows(own_row(rank_of(me)))] = packed[i, c, slot_rows(me)]

    each(pack, 3 * CHUNKS)

    for o in range(2):
        message(0, o).start()

    def pass_on(i, s, c):
        for rank in range(START[s], START[s] + SPLIT[s]):

            @pl.when(source(rank) != me)
            def _():
                dispatch_from(i, c, rank).wait_recv()

        mate_copy(i, s, c).start()

    each(lambda n: pass_on(order(n // CHUNKS), 0, n % CHUNKS), CHUNKS * (2 - core))

    most = max(SPLIT)
    for q in range(EXTRA):
        r = iota((2 * most * EXTRA, 2 * most * SLOTS), 0)
        i = iota((2 * most * EXTRA, 2 * most * SLOTS), 1)
        unfold[q] = (i == (r // EXTRA) * SLOTS + q * EXTRA + r % EXTRA).astype(F32).astype(BF16)
        r = iota((2 * most * SLOTS, 2 * most * EXTRA), 1)
        i = iota((2 * most * SLOTS, 2 * most * EXTRA), 0)
        fold[q] = (i == (r // EXTRA) * SLOTS + q * EXTRA + r % EXTRA).astype(F32).astype(BF16)

    for o in range(2):
        message(1, o).wait_recv()
        message(2, o).wait_recv()
        first, place = slots_of(far_route[o])
        whole = chosen(first, place, -1).T.astype(BF16)
        for q in range(EXTRA):
            sel_out[o, q, :, 0:main] = whole
            sel_out[o, q, :, main : 2 * main] = chosen(first, place, q).T.astype(BF16)
        prob[o] = jnp.broadcast_to(far_prob[o], (tok, tok)).T

    def sizes(s):
        block = SPLIT[s] * SLOTS
        extra = SPLIT[s] * EXTRA
        return block, 2 * extra, 2 * (block + extra)

    def load(i, s, c):
        block, extra, rows = sizes(s)
        stack[0 : 2 * block] = tokens[i, c, set_rows(s, 0, 2), 0:part]
        folded = tokens[i, c, set_rows(s, 0, 2), part:]
        for q in range(EXTRA):
            stack[2 * block : rows, q * quarter : (q + 1) * quarter] = dot(
                unfold[q, 0:extra, 0 : 2 * block], folded
            ).astype(BF16)
        return stack[0:rows]

    def store(o, s, c, value):
        block, extra, rows = sizes(s)
        at = part_rows(s)
        mine[o, c, at, 0:part] = value[0:block].astype(BF16)
        theirs[o, c, at, 0:part] = value[block : 2 * block].astype(BF16)
        rest = value[2 * block :].astype(BF16)
        total = dot(fold[0, 0 : 2 * block, 0:extra], rest[:, 0:quarter])
        for q in range(1, EXTRA):
            total += dot(fold[q, 0 : 2 * block, 0:extra], rest[:, q * quarter : (q + 1) * quarter])
        mine[o, c, at, part:] = total[0:block].astype(BF16)
        theirs[o, c, at, part:] = total[block:].astype(BF16)
        result_copy(o, s, c).start()

    def project(i, s, c):
        rows = pl.ds(0, sizes(s)[2])
        value = load(i, s, c)
        for half in range(2):
            at = pl.ds(half * hdev, hdev)
            acc[2 * i, rows, at] += dot(value, gate[half, cols(c)])
            acc[2 * i + 1, rows, at] += dot(value, up[half, cols(c)])

    def forward_in_step(s, c):
        mate_copy(0, s, c).wait_recv()
        project(0, s, c)

    def activate(s):
        rows = pl.ds(0, sizes(s)[2])
        gate_pre = acc[0, rows]
        hidden[rows] = (gate_pre / (1.0 + jnp.exp(-gate_pre)) * acc[1, rows]).astype(BF16)

    def backward_in_step(s, c):
        mate_copy(1, s, c).wait_recv()
        project(1, s, c)

    def down_step(s, c):
        store(0, s, c, dot(hidden[pl.ds(0, sizes(s)[2])], down[c]))

    def cot_step(s, c):
        mate_copy(2, s, c).wait_recv()
        acc[4, pl.ds(0, sizes(s)[2])] += dot_last(load(2, s, c), down[c])

    def differentiate(s):
        rows = pl.ds(0, sizes(s)[2])
        back_gate = acc[2, rows]
        back_hid = acc[4, rows]
        g = 1.0 / (1.0 + jnp.exp(-back_gate))
        grads[0, rows] = (back_hid * acc[3, rows] * g * (1.0 + back_gate * (1.0 - g))).astype(BF16)
        grads[1, rows] = (back_hid * back_gate * g).astype(BF16)

    def backward_step(s, c):
        rows = pl.ds(0, sizes(s)[2])
        total = dot_last(grads[0, rows, 0:hdev], gate[0, cols(c)])
        total += dot_last(grads[0, rows, hdev:], gate[1, cols(c)])
        total += dot_last(grads[1, rows, 0:hdev], up[0, cols(c)])
        total += dot_last(grads[1, rows, hdev:], up[1, cols(c)])
        store(1, s, c, total)

    def return_step(o, s, c):
        at = part_rows(s)
        result_copy(o, s, c).wait_recv()
        summed[o, c, at] = (mine[o, c, at].astype(F32) + others[o, c, at].astype(F32)).astype(BF16)
        for rank in range(START[s], START[s] + SPLIT[s]):
            give(o, c, rank).start()

    def finish(o, c):
        for j in range(experts):
            give_from(o, c, j).wait_recv()
        scale = jnp.concatenate([prob[o]] * (quarter // tok), axis=1)
        for q in range(EXTRA):
            at = pl.ds(multiple(c * part + q * quarter, quarter), quarter)
            branch = dot(sel_out[o, q, :, 0:main], back[o, c, :, q * quarter : (q + 1) * quarter])
            branch += dot(sel_out[o, q, :, main:], back[o, c, :, part:])
            value = resid[o, :, at].astype(F32) + scale * branch
            final[o, c, :, q * quarter : (q + 1) * quarter] = value.astype(BF16)
        out_copy(o, c).start()

    acc[...] = jnp.zeros_like(acc)
    def follow(c, body):
        @pl.when(c > 0)
        def _():
            body(c - 1)

    def arrived(i, c):
        weight_copy(i, c).wait_recv()

    def late_tokens(first, last):
        each(lambda n: pass_on(first + n // CHUNKS, 0, n % CHUNKS), CHUNKS * (last - first))

    def forward(first):
        def into(c):
            if first:
                arrived(0, c)
                arrived(1, c)
            forward_in_step(0, c)

        def out(c):
            if first:
                arrived(2, c)
                for at, i in LATE:

                    @pl.when(c == at)
                    def _():
                        late_tokens(i, i + 1)

            down_step(0, c)
            follow(c, lambda before: return_step(0, 0, before))

        each(into)
        activate(0)
        each(out)

    def backward(first):
        def into(c):
            if first:
                arrived(0, c)
                arrived(1, c)
            backward_in_step(0, c)

        def against(c):
            if first:
                arrived(2, c)
            cot_step(0, c)

        def out(c):
            backward_step(0, c)
            follow(c, lambda before: return_step(1, 0, before))

        each(into)
        each(against)
        if first:
            late_tokens(0, 1)
        differentiate(0)
        each(out)

    @pl.when(core == 1)
    def _():
        forward(True)
        return_step(0, 0, CHUNKS - 1)
        backward(False)
        return_step(1, 0, CHUNKS - 1)

    @pl.when(core == 0)
    def _():
        backward(True)
        return_step(1, 0, CHUNKS - 1)
        forward(False)
        return_step(0, 0, CHUNKS - 1)

    for o in range(2):
        message(0, o).wait_recv()

    @pl.when(core == 0)
    def _():
        each(lambda c: finish(0, c))
        each(lambda c: finish(1, c))

    @pl.when(core == 1)
    def _():
        each(lambda c: finish(1, c))
        each(lambda c: finish(0, c))

    def drain(c):
        for i in range(3):
            weight_copy(i, c).wait_send()
            for s in range(SETS):
                mate_copy(i, s, c).wait_send()
            for k in range(1, experts):
                dispatch(i, c, k).wait_send()
        for o in range(2):
            for s in range(SETS):
                result_copy(o, s, c).wait_send()
            for rank in range(experts):
                give(o, c, rank).wait_send()
            out_copy(o, c).wait()

    each(drain)
    for i in range(3):
        for o in range(2):
            message(i, o).wait_send()


def on_device(
    forward_in,
    forward_route,
    forward_gate_prob,
    backward_in,
    backward_route,
    backward_gate_prob,
    cotangent,
    w_gate,
    w_up,
    w_down,
):
    experts = lax.axis_size("expert") // GROUP
    pipes = lax.axis_size("pipe")
    _, tok, width = forward_in.shape
    hdev = w_gate.shape[2]
    main = experts * SLOTS
    block = max(SPLIT) * SLOTS
    extra = max(SPLIT) * EXTRA
    part = width // CHUNKS
    wide = part + part // EXTRA
    rows = 2 * (block + extra)
    hbm = pl.BlockSpec(memory_space=pl.ANY)
    vmem = pl.BlockSpec(memory_space=pltpu.VMEM)
    dma = pltpu.SemaphoreType.DMA
    return pl.pallas_call(
        functools.partial(kernel, experts, pipes),
        out_shape=[jax.ShapeDtypeStruct(forward_in.shape, BF16)] * 2,
        in_specs=[hbm] * 6 + [vmem] * 4,
        out_specs=[hbm] * 2,
        scratch_shapes=[
            pltpu.VMEM((3, tok, width), BF16),
            pltpu.VMEM((3, CHUNKS, main, wide), BF16),
            pltpu.VMEM((3, CHUNKS, 2 * main, wide), BF16),
            pltpu.VMEM((2, width, hdev), BF16),
            pltpu.VMEM((2, width, hdev), BF16),
            pltpu.VMEM((CHUNKS, 2 * hdev, part), BF16),
            pltpu.VMEM((rows, part), BF16),
            pltpu.VMEM((5, rows, 2 * hdev), F32),
            pltpu.VMEM((rows, 2 * hdev), BF16),
            pltpu.VMEM((2, rows, 2 * hdev), BF16),
            pltpu.VMEM((2, CHUNKS, main, wide), BF16),
            pltpu.VMEM((2, CHUNKS, main, wide), BF16),
            pltpu.VMEM((2, CHUNKS, main, wide), BF16),
            pltpu.VMEM((2, CHUNKS, main, wide), BF16),
            pltpu.VMEM((2, CHUNKS, main, wide), BF16),
            pltpu.VMEM((2, tok, width), BF16),
            pltpu.VMEM((2, 1, tok), jnp.int32),
            pltpu.VMEM((2, 1, tok), F32),
            pltpu.VMEM((2, tok, tok), F32),
            pltpu.VMEM((2, CHUNKS, tok, part), BF16),
            pltpu.VMEM((2, 1 + EXTRA, main, tok), BF16),
            pltpu.VMEM((2, EXTRA, tok, 2 * main), BF16),
            pltpu.VMEM((EXTRA, 2 * extra, 2 * block), BF16),
            pltpu.VMEM((EXTRA, 2 * block, 2 * extra), BF16),
            dma((5 + CHUNKS,)),
            dma((3, CHUNKS)),
            dma((3, CHUNKS)),
            dma((3, CHUNKS, experts)),
            dma((3, CHUNKS, experts)),
            dma((3, SETS, CHUNKS)),
            dma((3, SETS, CHUNKS)),
            dma((2, SETS, CHUNKS)),
            dma((2, SETS, CHUNKS)),
            dma((2, CHUNKS, experts)),
            dma((2, CHUNKS, experts)),
            dma((3, 2)),
            dma((3, 2)),
            dma((2, CHUNKS)),
        ],
        compiler_params=pltpu.CompilerParams(
            collective_id=1, has_side_effects=True, vmem_limit_bytes=60 * 2**20
        ),
    )(
        forward_in,
        backward_in,
        cotangent,
        w_gate,
        w_up,
        w_down,
        forward_route.reshape(1, tok),
        backward_route.reshape(1, tok),
        forward_gate_prob.reshape(1, tok),
        backward_gate_prob.reshape(1, tok),
    )


def solution(mesh):
    tokens = P("pipe", "expert", None)
    columns = P("pipe", None, "expert")
    return jax.shard_map(
        lambda *args: tuple(on_device(*args)),
        mesh=mesh,
        in_specs=(tokens,) * 7 + (columns, columns, tokens),
        out_specs=(tokens, tokens),
        check_vma=False,
    )
```

```python
import functools

import jax
import jax.numpy as jnp
from jax import lax
from jax.experimental import pallas as pl
from jax.experimental.pallas import tpu as pltpu
from jax.sharding import PartitionSpec as P

MESH = pl.DeviceIdType.MESH
F32 = jnp.float32
BF16 = jnp.bfloat16

GROUP = 4
SLOTS = 16
EXTRA = 4
CHUNKS = 4
SPLIT = (8,)
SETS = len(SPLIT)
LATE = ((0, 1), (2, 2))
START = tuple(sum(SPLIT[:s]) for s in range(SETS))


def dot(left, right):
    return jnp.dot(left, right, preferred_element_type=F32)


def dot_last(left, right):
    return lax.dot_general(left, right, (((1,), (1,)), ((), ())), preferred_element_type=F32)


def iota(shape, dim):
    return lax.broadcasted_iota(jnp.int32, shape, dim)


def multiple(value, of):
    return pl.multiple_of(value, of)


def kernel(
    experts,
    pipes,
    fwd_in,
    bwd_in,
    cot_in,
    w_gate,
    w_up,
    w_down,
    fwd_route,
    bwd_route,
    fwd_prob,
    bwd_prob,
    next_fwd,
    next_cot,
    rows_in,
    packed,
    tokens,
    gate,
    up,
    down,
    stack,
    acc,
    hidden,
    grads,
    mine,
    theirs,
    others,
    summed,
    back,
    resid,
    far_route,
    far_prob,
    prob,
    final,
    sel_in,
    sel_out,
    unfold,
    fold,
    local_sem,
    w_send,
    w_recv,
    d_send,
    d_recv,
    t_send,
    t_recv,
    c_send,
    c_recv,
    r_send,
    r_recv,
    m_send,
    m_recv,
    out_sem,
):
    tok, width = rows_in.shape[1], rows_in.shape[2]
    part = width // CHUNKS
    quarter = part // EXTRA
    hdev = gate.shape[2]
    main = experts * SLOTS

    section = lax.axis_index("pipe")
    member = lax.axis_index("expert")
    core = section % 2
    x = member % GROUP
    me = member // GROUP
    pair_a = x + 1 - 2 * (x % 2)
    pair_b = GROUP - 1 - x
    token_mate = (section, me * GROUP + (1 - core) * pair_a + core * pair_b)
    weight_mate = (section, me * GROUP + core * pair_a + (1 - core) * pair_b)
    ahead = (section + 1) % pipes
    behind = (section + pipes - 1) % pipes

    def peer(k):
        return (me + k) % experts

    def rank_of(j):
        z = j // 4
        return (j + 2 * z + 3) % 4 * 2 + z

    def source(rank):
        z = rank % 2
        return z * 4 + (rank // 2 + 1 + 2 * z) % 4

    def own_row(rank):
        return rank + START[-1] * (rank // SPLIT[0])

    def remote(src, dst, send, recv, device):
        return pltpu.make_async_remote_copy(
            src_ref=src, dst_ref=dst, send_sem=send, recv_sem=recv, device_id=device, device_id_type=MESH
        )

    def cols(c):
        return pl.ds(multiple(c * part, part), part)

    def slot_rows(k):
        return pl.ds(multiple(k * SLOTS, SLOTS), SLOTS)

    def weight_copy(i, c):
        if i < 2:
            held = (gate, up)[i]
            return remote(
                held.at[0, cols(c)], held.at[1, cols(c)], w_send.at[i, c], w_recv.at[i, c], weight_mate
            )
        return remote(
            down.at[c, pl.ds(0, hdev)],
            down.at[c, pl.ds(hdev, hdev)],
            w_send.at[i, c],
            w_recv.at[i, c],
            weight_mate,
        )

    def set_rows(s, side=0, count=1):
        return pl.ds((2 * START[s] + side * SPLIT[s]) * SLOTS, count * SPLIT[s] * SLOTS)

    def part_rows(s):
        return pl.ds(START[s] * SLOTS, SPLIT[s] * SLOTS)

    def dispatch(i, c, k):
        to = peer(k)
        return remote(
            packed.at[i, c, slot_rows(to)],
            tokens.at[i, c, slot_rows(own_row(rank_of(me)))],
            d_send.at[i, c, k],
            d_recv.at[i, c, me],
            (section, to * GROUP + x),
        )

    def dispatch_from(i, c, rank):
        j = source(rank)
        return remote(
            packed.at[i, c, slot_rows(j)],
            tokens.at[i, c, slot_rows(own_row(rank))],
            d_send.at[i, c, 0],
            d_recv.at[i, c, j],
            (section, j * GROUP + x),
        )

    def mate_copy(i, s, c):
        return remote(
            tokens.at[i, c, set_rows(s)],
            tokens.at[i, c, set_rows(s, 1)],
            t_send.at[i, s, c],
            t_recv.at[i, s, c],
            token_mate,
        )

    def result_copy(o, s, c):
        return remote(
            theirs.at[o, c, part_rows(s)],
            others.at[o, c, part_rows(s)],
            c_send.at[o, s, c],
            c_recv.at[o, s, c],
            token_mate,
        )

    def give(o, c, rank):
        j = source(rank)
        return remote(
            summed.at[o, c, slot_rows(rank)],
            back.at[o, c, slot_rows(me)],
            r_send.at[o, c, j],
            r_recv.at[o, c, me],
            ((ahead, behind)[o], j * GROUP + x),
        )

    def give_from(o, c, j):
        return remote(
            summed.at[o, c, slot_rows(0)],
            back.at[o, c, slot_rows(j)],
            r_send.at[o, c, j],
            r_recv.at[o, c, j],
            ((ahead, behind)[o], j * GROUP + x),
        )

    def message(i, o):
        src, dst = (
            ((fwd_in, cot_in)[o].at[0], resid.at[o]),
            ((fwd_route, bwd_route)[o], far_route.at[o]),
            ((fwd_prob, bwd_prob)[o], far_prob.at[o]),
        )[i]
        return remote(src, dst, m_send.at[i, o], m_recv.at[i, o], ((ahead, behind)[o], member))

    def out_copy(o, c):
        out = (next_fwd, next_cot)[o]
        return pltpu.make_async_copy(final.at[o, c], out.at[0, :, cols(c)], out_sem.at[o, c])

    def each(body, count=CHUNKS):
        lax.fori_loop(0, count, lambda c, carry: (body(c), carry)[1], 0)

    local = [
        pltpu.make_async_copy(src.at[0], rows_in.at[i], local_sem.at[i])
        for i, src in enumerate((fwd_in, bwd_in, cot_in))
    ]
    local.append(pltpu.make_async_copy(w_gate.at[0], gate.at[0], local_sem.at[3]))
    local.append(pltpu.make_async_copy(w_up.at[0], up.at[0], local_sem.at[4]))
    for c in range(CHUNKS):
        local.append(
            pltpu.make_async_copy(
                w_down.at[0, :, pl.ds(c * part, part)], down.at[c, pl.ds(0, hdev)], local_sem.at[5 + c]
            )
        )
    for copy in local[3:5] + local[:3] + local[5:]:
        copy.start()

    barrier = pltpu.get_barrier_semaphore()

    def greet(device):
        pl.semaphore_signal(barrier, inc=1, device_id=device, device_id_type=MESH)

    greet(token_mate)
    greet(weight_mate)
    each(lambda k: greet((section, peer(k + 1) * GROUP + x)), experts - 1)
    each(lambda k: greet((ahead, k * GROUP + x)), experts)
    each(lambda k: greet((behind, k * GROUP + x)), experts)

    pl.semaphore_wait(barrier, 2 + (experts - 1) + 2 * experts)
    for i in range(3):
        for copy in (local[3:4], local[4:5], local[5:])[i]:
            copy.wait()
        each(lambda c: weight_copy(i, c).start())

    def slots_of(route):
        onehot = (iota((SLOTS, tok), 0) == route).astype(F32)
        earlier = (iota((tok, tok), 0) < iota((tok, tok), 1)).astype(F32).astype(BF16)
        before = dot(onehot.astype(BF16), earlier)
        place = jnp.sum(before * onehot, axis=0, keepdims=True)
        return route.astype(F32) * SLOTS, place

    def chosen(first, place, q):
        if q < 0:
            slot = jnp.where(place < SLOTS, first + place, -1.0)
        else:
            slot = jnp.where(place >= SLOTS, first + (place - SLOTS) + q * EXTRA, -1.0)
        return (slot == iota((main, tok), 0).astype(F32)).astype(F32)

    for o in range(2):
        first, place = slots_of((fwd_route, bwd_route)[o][...])
        for q in range(1 + EXTRA):
            sel_in[o, q] = chosen(first, place, q - 1).astype(BF16)

    for o in range(2):
        message(1, o).start()
        message(2, o).start()

    for copy in local[0:3]:
        copy.wait()

    def order(k):
        return (k + 1 - core) % 3

    def pack(n):
        i, c = order(n // CHUNKS), n % CHUNKS
        o = (i + 1) // 2
        rows = rows_in.at[i, :, cols(c)]
        packed[i, c, :, 0:part] = dot(sel_in[o, 0], rows[...]).astype(BF16)
        total = dot(sel_in[o, 1], rows[:, 0:quarter])
        for q in range(1, EXTRA):
            total += dot(sel_in[o, 1 + q], rows[:, q * quarter : (q + 1) * quarter])
        packed[i, c, :, part:] = total.astype(BF16)
        for k in range(1, experts):
            dispatch(i, c, k).start()
        tokens[i, c, slot_rows(own_row(rank_of(me)))] = packed[i, c, slot_rows(me)]

    each(pack, 3 * CHUNKS)

    for o in range(2):
        message(0, o).start()

    def pass_on(i, s, c):
        for rank in range(START[s], START[s] + SPLIT[s]):

            @pl.when(source(rank) != me)
            def _():
                dispatch_from(i, c, rank).wait_recv()

        mate_copy(i, s, c).start()

    each(lambda n: pass_on(order(n // CHUNKS), 0, n % CHUNKS), CHUNKS * (2 - core))

    most = max(SPLIT)
    for q in range(EXTRA):
        r = iota((2 * most * EXTRA, 2 * most * SLOTS), 0)
        i = iota((2 * most * EXTRA, 2 * most * SLOTS), 1)
        unfold[q] = (i == (r // EXTRA) * SLOTS + q * EXTRA + r % EXTRA).astype(F32).astype(BF16)
        r = iota((2 * most * SLOTS, 2 * most * EXTRA), 1)
        i = iota((2 * most * SLOTS, 2 * most * EXTRA), 0)
        fold[q] = (i == (r // EXTRA) * SLOTS + q * EXTRA + r % EXTRA).astype(F32).astype(BF16)

    for o in range(2):
        message(1, o).wait_recv()
        message(2, o).wait_recv()
        first, place = slots_of(far_route[o])
        whole = chosen(first, place, -1).T.astype(BF16)
        for q in range(EXTRA):
            sel_out[o, q, :, 0:main] = whole
            sel_out[o, q, :, main : 2 * main] = chosen(first, place, q).T.astype(BF16)
        prob[o] = jnp.broadcast_to(far_prob[o], (tok, tok)).T

    def sizes(s):
        block = SPLIT[s] * SLOTS
        extra = SPLIT[s] * EXTRA
        return block, 2 * extra, 2 * (block + extra)

    def load(i, s, c):
        block, extra, rows = sizes(s)
        stack[0 : 2 * block] = tokens[i, c, set_rows(s, 0, 2), 0:part]
        folded = tokens[i, c, set_rows(s, 0, 2), part:]
        for q in range(EXTRA):
            stack[2 * block : rows, q * quarter : (q + 1) * quarter] = dot(
                unfold[q, 0:extra, 0 : 2 * block], folded
            ).astype(BF16)
        return stack[0:rows]

    def store(o, s, c, value):
        block, extra, rows = sizes(s)
        at = part_rows(s)
        mine[o, c, at, 0:part] = value[0:block].astype(BF16)
        theirs[o, c, at, 0:part] = value[block : 2 * block].astype(BF16)
        rest = value[2 * block :].astype(BF16)
        total = dot(fold[0, 0 : 2 * block, 0:extra], rest[:, 0:quarter])
        for q in range(1, EXTRA):
            total += dot(fold[q, 0 : 2 * block, 0:extra], rest[:, q * quarter : (q + 1) * quarter])
        mine[o, c, at, part:] = total[0:block].astype(BF16)
        theirs[o, c, at, part:] = total[block:].astype(BF16)
        result_copy(o, s, c).start()

    def project(i, s, c):
        rows = pl.ds(0, sizes(s)[2])
        value = load(i, s, c)
        for half in range(2):
            at = pl.ds(half * hdev, hdev)
            acc[2 * i, rows, at] += dot(value, gate[half, cols(c)])
            acc[2 * i + 1, rows, at] += dot(value, up[half, cols(c)])

    def forward_in_step(s, c):
        mate_copy(0, s, c).wait_recv()
        project(0, s, c)

    def activate(s):
        rows = pl.ds(0, sizes(s)[2])
        gate_pre = acc[0, rows]
        hidden[rows] = (gate_pre / (1.0 + jnp.exp(-gate_pre)) * acc[1, rows]).astype(BF16)

    def backward_in_step(s, c):
        mate_copy(1, s, c).wait_recv()
        project(1, s, c)

    def down_step(s, c):
        store(0, s, c, dot(hidden[pl.ds(0, sizes(s)[2])], down[c]))

    def cot_step(s, c):
        mate_copy(2, s, c).wait_recv()
        acc[4, pl.ds(0, sizes(s)[2])] += dot_last(load(2, s, c), down[c])

    def differentiate(s):
        rows = pl.ds(0, sizes(s)[2])
        back_gate = acc[2, rows]
        back_hid = acc[4, rows]
        g = 1.0 / (1.0 + jnp.exp(-back_gate))
        grads[0, rows] = (back_hid * acc[3, rows] * g * (1.0 + back_gate * (1.0 - g))).astype(BF16)
        grads[1, rows] = (back_hid * back_gate * g).astype(BF16)

    def backward_step(s, c):
        rows = pl.ds(0, sizes(s)[2])
        total = dot_last(grads[0, rows, 0:hdev], gate[0, cols(c)])
        total += dot_last(grads[0, rows, hdev:], gate[1, cols(c)])
        total += dot_last(grads[1, rows, 0:hdev], up[0, cols(c)])
        total += dot_last(grads[1, rows, hdev:], up[1, cols(c)])
        store(1, s, c, total)

    def return_step(o, s, c):
        at = part_rows(s)
        result_copy(o, s, c).wait_recv()
        summed[o, c, at] = (mine[o, c, at].astype(F32) + others[o, c, at].astype(F32)).astype(BF16)
        for rank in range(START[s], START[s] + SPLIT[s]):
            give(o, c, rank).start()

    def finish(o, c):
        for j in range(experts):
            give_from(o, c, j).wait_recv()
        scale = jnp.concatenate([prob[o]] * (quarter // tok), axis=1)
        for q in range(EXTRA):
            at = pl.ds(multiple(c * part + q * quarter, quarter), quarter)
            branch = dot(sel_out[o, q, :, 0:main], back[o, c, :, q * quarter : (q + 1) * quarter])
            branch += dot(sel_out[o, q, :, main:], back[o, c, :, part:])
            value = resid[o, :, at].astype(F32) + scale * branch
            final[o, c, :, q * quarter : (q + 1) * quarter] = value.astype(BF16)
        out_copy(o, c).start()

    acc[...] = jnp.zeros_like(acc)
    def follow(c, body):
        @pl.when(c > 0)
        def _():
            body(c - 1)

    def arrived(i, c):
        weight_copy(i, c).wait_recv()

    def late_tokens(first, last):
        each(lambda n: pass_on(first + n // CHUNKS, 0, n % CHUNKS), CHUNKS * (last - first))

    def forward(first):
        def into(c):
            if first:
                arrived(0, c)
                arrived(1, c)
            forward_in_step(0, c)

        def out(c):
            if first:
                arrived(2, c)
                for at, i in LATE:

                    @pl.when(c == at)
                    def _():
                        late_tokens(i, i + 1)

            down_step(0, c)
            follow(c, lambda before: return_step(0, 0, before))

        each(into)
        activate(0)
        each(out)

    def backward(first):
        def into(c):
            if first:
                arrived(0, c)
                arrived(1, c)
            backward_in_step(0, c)

        def against(c):
            if first:
                arrived(2, c)

                @pl.when(c == CHUNKS - 1)
                def _():
                    late_tokens(0, 1)

            cot_step(0, c)

        def out(c):
            backward_step(0, c)
            follow(c, lambda before: return_step(1, 0, before))

        each(into)
        each(against)
        differentiate(0)
        each(out)

    @pl.when(core == 1)
    def _():
        forward(True)
        return_step(0, 0, CHUNKS - 1)
        backward(False)
        return_step(1, 0, CHUNKS - 1)

    @pl.when(core == 0)
    def _():
        backward(True)
        return_step(1, 0, CHUNKS - 1)
        forward(False)
        return_step(0, 0, CHUNKS - 1)

    for o in range(2):
        message(0, o).wait_recv()

    @pl.when(core == 0)
    def _():
        each(lambda c: finish(0, c))
        each(lambda c: finish(1, c))

    @pl.when(core == 1)
    def _():
        each(lambda c: finish(1, c))
        each(lambda c: finish(0, c))

    def drain(c):
        for i in range(3):
            weight_copy(i, c).wait_send()
            for s in range(SETS):
                mate_copy(i, s, c).wait_send()
            for k in range(1, experts):
                dispatch(i, c, k).wait_send()
        for o in range(2):
            for s in range(SETS):
                result_copy(o, s, c).wait_send()
            for rank in range(experts):
                give(o, c, rank).wait_send()
            out_copy(o, c).wait()

    each(drain)
    for i in range(3):
        for o in range(2):
            message(i, o).wait_send()


def on_device(
    forward_in,
    forward_route,
    forward_gate_prob,
    backward_in,
    backward_route,
    backward_gate_prob,
    cotangent,
    w_gate,
    w_up,
    w_down,
):
    experts = lax.axis_size("expert") // GROUP
    pipes = lax.axis_size("pipe")
    _, tok, width = forward_in.shape
    hdev = w_gate.shape[2]
    main = experts * SLOTS
    block = max(SPLIT) * SLOTS
    extra = max(SPLIT) * EXTRA
    part = width // CHUNKS
    wide = part + part // EXTRA
    rows = 2 * (block + extra)
    hbm = pl.BlockSpec(memory_space=pl.ANY)
    vmem = pl.BlockSpec(memory_space=pltpu.VMEM)
    dma = pltpu.SemaphoreType.DMA
    return pl.pallas_call(
        functools.partial(kernel, experts, pipes),
        out_shape=[jax.ShapeDtypeStruct(forward_in.shape, BF16)] * 2,
        in_specs=[hbm] * 6 + [vmem] * 4,
        out_specs=[hbm] * 2,
        scratch_shapes=[
            pltpu.VMEM((3, tok, width), BF16),
            pltpu.VMEM((3, CHUNKS, main, wide), BF16),
            pltpu.VMEM((3, CHUNKS, 2 * main, wide), BF16),
            pltpu.VMEM((2, width, hdev), BF16),
            pltpu.VMEM((2, width, hdev), BF16),
            pltpu.VMEM((CHUNKS, 2 * hdev, part), BF16),
            pltpu.VMEM((rows, part), BF16),
            pltpu.VMEM((5, rows, 2 * hdev), F32),
            pltpu.VMEM((rows, 2 * hdev), BF16),
            pltpu.VMEM((2, rows, 2 * hdev), BF16),
            pltpu.VMEM((2, CHUNKS, main, wide), BF16),
            pltpu.VMEM((2, CHUNKS, main, wide), BF16),
            pltpu.VMEM((2, CHUNKS, main, wide), BF16),
            pltpu.VMEM((2, CHUNKS, main, wide), BF16),
            pltpu.VMEM((2, CHUNKS, main, wide), BF16),
            pltpu.VMEM((2, tok, width), BF16),
            pltpu.VMEM((2, 1, tok), jnp.int32),
            pltpu.VMEM((2, 1, tok), F32),
            pltpu.VMEM((2, tok, tok), F32),
            pltpu.VMEM((2, CHUNKS, tok, part), BF16),
            pltpu.VMEM((2, 1 + EXTRA, main, tok), BF16),
            pltpu.VMEM((2, EXTRA, tok, 2 * main), BF16),
            pltpu.VMEM((EXTRA, 2 * extra, 2 * block), BF16),
            pltpu.VMEM((EXTRA, 2 * block, 2 * extra), BF16),
            dma((5 + CHUNKS,)),
            dma((3, CHUNKS)),
            dma((3, CHUNKS)),
            dma((3, CHUNKS, experts)),
            dma((3, CHUNKS, experts)),
            dma((3, SETS, CHUNKS)),
            dma((3, SETS, CHUNKS)),
            dma((2, SETS, CHUNKS)),
            dma((2, SETS, CHUNKS)),
            dma((2, CHUNKS, experts)),
            dma((2, CHUNKS, experts)),
            dma((3, 2)),
            dma((3, 2)),
            dma((2, CHUNKS)),
        ],
        compiler_params=pltpu.CompilerParams(
            collective_id=1, has_side_effects=True, vmem_limit_bytes=60 * 2**20
        ),
    )(
        forward_in,
        backward_in,
        cotangent,
        w_gate,
        w_up,
        w_down,
        forward_route.reshape(1, tok),
        backward_route.reshape(1, tok),
        forward_gate_prob.reshape(1, tok),
        backward_gate_prob.reshape(1, tok),
    )


def solution(mesh):
    tokens = P("pipe", "expert", None)
    columns = P("pipe", None, "expert")
    return jax.shard_map(
        lambda *args: tuple(on_device(*args)),
        mesh=mesh,
        in_specs=(tokens,) * 7 + (columns, columns, tokens),
        out_specs=(tokens, tokens),
        check_vma=False,
    )
```
